32 devices in a mesh: ctx: 8 (over z, y), chan: 4 (over x, core).
Axes of the slice: x: 2, y: 2, z: 4, core: 2. Of those that a mesh axis runs over, the one named last changes fastest.
Arguments:
- layer_in: float32 [1024, 8192], P('ctx', 'chan'), may hold values from -64 to 64
- query_mr: float32 [1024, 8192], P('ctx', 'chan'), may hold values from -6 to 6
- key_mr: float32 [1024, 8192], P('ctx', 'chan'), may hold values from -6 to 6
- query_lr: float32 [1024, 8192], P('ctx', 'chan'), may hold values from -6 to 6
- key_lr: float32 [1024, 8192], P('ctx', 'chan'), may hold values from -6 to 6
- filter_mr: float32 [128, 8192], P(None, 'chan'), may hold values from -0.5 to 0.5
- filter_lr: float32 [1024, 8192], P('ctx', 'chan'), may hold values from -0.1875 to 0.1875
- norm_gain: float32 [8192], P('chan'), may hold values from 0.1 to 1.9
- out_grad: float32 [1024, 8192], P('ctx', 'chan'), may hold values from -6 to 6
Outputs:
- grad_in: float32 [1024, 8192], P('ctx', 'chan')
- grad_query_mr: float32 [1024, 8192], P('ctx', 'chan')
- grad_key_mr: float32 [1024, 8192], P('ctx', 'chan')
- grad_filter_mr: float32 [128, 8192], P(None, 'chan')
- grad_gain: float32 [8192], P('chan')
- grad_query_lr: float32 [1024, 8192], P('ctx', 'chan')
- grad_key_lr: float32 [1024, 8192], P('ctx', 'chan')
- grad_filter_lr: float32 [1024, 8192], P('ctx', 'chan')
The draws below stay inside these ranges and needn't reach their ends.
All inputs are finite; a program needn't handle non-finite values.
Results may differ from the reference program's by a relative error of at most 0.0003.
Values sent between devices are 32-bit elements; how exact they have to be, the bound alone decides.
A program may use at most 128 MiB of HBM per device.

```python
import math
import jax
import jax.numpy as jnp
from jax import lax

D = 8192
TAPS = 128
TOKENS = 1024


def draw_layer_in(key, part):
    key_base = jax.random.fold_in(key, 11)
    key_rows = jax.random.fold_in(key, 12)
    key_cols = jax.random.fold_in(key, 13)
    base = jnp.clip(jax.random.normal(key_base, (TOKENS, D), jnp.float32), -6.0, 6.0)
    row_scale = jnp.exp(jax.random.uniform(key_rows, (TOKENS, 1), jnp.float32, math.log(0.3), math.log(3.0)))
    ramp = jnp.arange(D, dtype=jnp.float32) / D
    col_scale = jnp.exp(math.log(3.0) * (ramp - 0.5) + jax.random.uniform(key_cols, (D,), jnp.float32, -0.6, 0.6))
    return base * row_scale * col_scale[None, :]


def block_levels(stream_key, shape, cuts, low, top_value):
    loudness, own = 1.0, jax.random.fold_in(stream_key, 6)
    for position, parts in cuts:
        draws = jnp.exp(jax.random.uniform(jax.random.fold_in(own, position), (parts,), jnp.float32, low / len(cuts), top_value / len(cuts)))
        loudness = loudness * jnp.repeat(draws, shape[position] // parts).reshape([-1 if axis == position else 1 for axis in range(len(shape))])
    return loudness


def gaussian(stream_key, shape, width, most, shards=(), kind=jnp.bfloat16):
    level = block_levels(stream_key, shape, shards, -0.22, 0.18) if shards else 1.0
    values = jax.random.normal(stream_key, shape, jnp.float32) * width * level
    return jnp.minimum(jnp.maximum(values, -most), most).astype(kind)


def setup_inputs(seed: int = 0) -> dict:
    streams_of = jax.random.split(jax.random.key(seed), 10)
    return {
        "layer_in": draw_layer_in(jax.random.fold_in(streams_of[9], 71), 0),
        "query_mr": gaussian(streams_of[1], (TOKENS, D), 1.0, 6.0, ((0, 8), (1, 4)), jnp.float32),
        "key_mr": gaussian(streams_of[2], (TOKENS, D), 1.0, 6.0, ((0, 8), (1, 4)), jnp.float32),
        "query_lr": gaussian(streams_of[3], (TOKENS, D), 1.0, 6.0, ((0, 8), (1, 4)), jnp.float32),
        "key_lr": gaussian(streams_of[4], (TOKENS, D), 1.0, 6.0, ((0, 8), (1, 4)), jnp.float32),
        "filter_mr": gaussian(streams_of[5], (TAPS, D), TAPS ** -0.5, 0.5, ((1, 4),), jnp.float32),
        "filter_lr": gaussian(streams_of[6], (TOKENS, D), TOKENS ** -0.5, 0.1875, ((0, 8), (1, 4)), jnp.float32),
        "norm_gain": jnp.clip(1.0 + 0.18 * jax.random.normal(streams_of[7], (D,), jnp.float32), 0.1, 1.9),
        "out_grad": gaussian(streams_of[8], (TOKENS, D), 1.0, 6.0, ((0, 8), (1, 4)), jnp.float32),
    }


def causal_taps(extended, kernel, length):
    tap_count = kernel.shape[0]

    def add_tap(index, total):
        start = (tap_count - 1 - index).astype(jnp.int32)
        window = lax.dynamic_slice_in_dim(extended, start, length, 0)
        weight = lax.dynamic_slice_in_dim(kernel, index.astype(jnp.int32), 1, 0)
        return total + weight * window
    zeros = jnp.zeros((length, extended.shape[1]), jnp.float32)
    return lax.fori_loop(jnp.int32(0), jnp.int32(tap_count), add_tap, zeros)

def anti_taps(extended, kernel, length):
    tap_count = kernel.shape[0]

    def add_tap(index, total):
        window = lax.dynamic_slice_in_dim(extended, index.astype(jnp.int32), length, 0)
        weight = lax.dynamic_slice_in_dim(kernel, index.astype(jnp.int32), 1, 0)
        return total + weight * window
    zeros = jnp.zeros((length, extended.shape[1]), jnp.float32)
    return lax.fori_loop(jnp.int32(0), jnp.int32(tap_count), add_tap, zeros)

def tap_products(extended, grads, tap_count):
    length = grads.shape[0]

    def one_tap(index):
        start = (tap_count - 1 - index).astype(jnp.int32)
        window = lax.dynamic_slice_in_dim(extended, start, length, 0)
        return lax.optimization_barrier(jnp.sum(grads * window, axis=0))
    return lax.map(one_tap, jnp.arange(tap_count, dtype=jnp.int32))

def long_block(pieces):
    values, grad_pieces, filt_piece = pieces
    length = values.shape[1]
    padded = 2 * length
    spec_values = jnp.fft.rfft(values, n=padded, axis=1)
    spec_grads = jnp.fft.rfft(grad_pieces, n=padded, axis=1)
    spec_filter = jnp.fft.rfft(filt_piece, n=padded, axis=1)
    conv_full = jnp.fft.irfft(spec_values * spec_filter, n=padded, axis=1)[:, :length]
    back_full = jnp.fft.irfft(jnp.conj(spec_filter) * spec_grads, n=padded, axis=1)[:, :length]
    filter_full = jnp.fft.irfft(jnp.conj(spec_values) * spec_grads, n=padded, axis=1)[:, :length]
    return (conv_full, back_full, filter_full)

def reference(layer_in, query_mr, key_mr, query_lr, key_lr, filter_mr, filter_lr, norm_gain, out_grad):
    block_width = math.gcd(D, 256)

    def by_blocks(array):
        return array.T.reshape(D // block_width, block_width, TOKENS)

    def from_blocks(array):
        return array.reshape(D, TOKENS).T
    mixed_in = key_mr * layer_in
    mixed_ext = jnp.concatenate([jnp.zeros((TAPS - 1, D), jnp.float32), mixed_in], 0)
    conv_mr = causal_taps(mixed_ext, filter_mr, TOKENS)
    residual = layer_in + query_mr * conv_mr
    inv_rms = lax.rsqrt(lax.optimization_barrier(jnp.mean(residual * residual, axis=1)) + 1e-06)[:, None]
    normed = residual * inv_rms * norm_gain
    long_in = key_lr * normed
    grad_conv_lr = out_grad * query_lr
    conv_b, back_b, filt_b = lax.map(long_block, (by_blocks(long_in), by_blocks(grad_conv_lr), by_blocks(filter_lr)))
    conv_lr = from_blocks(conv_b)
    grad_long_in = from_blocks(back_b)
    grad_filter_lr = from_blocks(filt_b)
    grad_query_lr = out_grad * conv_lr
    grad_key_lr = grad_long_in * normed
    grad_normed = grad_long_in * key_lr
    grad_gain = lax.optimization_barrier(jnp.sum(grad_normed * residual * inv_rms, axis=0))
    scaled = norm_gain * grad_normed
    cross_mean = lax.optimization_barrier(jnp.mean(scaled * residual, axis=1))[:, None]
    grad_resid = out_grad + inv_rms * scaled - residual * inv_rms ** 3 * cross_mean
    grad_query_mr = grad_resid * conv_mr
    grad_conv_mr = grad_resid * query_mr
    grad_filter_mr = tap_products(mixed_ext, grad_conv_mr, TAPS)
    grad_ext = jnp.concatenate([grad_conv_mr, jnp.zeros((TAPS - 1, D), jnp.float32)], 0)
    grad_mixed = anti_taps(grad_ext, filter_mr, TOKENS)
    grad_key_mr = grad_mixed * layer_in
    grad_in = grad_resid + grad_mixed * key_mr
    return (grad_in, grad_query_mr, grad_key_mr, grad_filter_mr, grad_gain, grad_query_lr, grad_key_lr, grad_filter_lr)
```

```python
import math

import jax
import jax.numpy as jnp
import numpy as np
from jax import lax
from jax.sharding import PartitionSpec as P


def shifted(shard, axis, by):
    peers = lax.axis_size(axis)
    pairs = [(i, i + by) for i in range(peers) if 0 <= i + by < peers]
    return lax.ppermute(shard, axis, pairs)


def mult_in(form, left, right):
    return jnp.einsum(form, left, right, precision=lax.Precision.HIGHEST)


def dft_tables(half_rows):
    freq_rows = 2 * half_rows
    grid_total = freq_rows * 128
    first_freq = jnp.arange(freq_rows, dtype=jnp.int32)
    first_half = jnp.arange(half_rows, dtype=jnp.int32)
    second_idx = jnp.arange(128, dtype=jnp.int32)
    angle_one = (first_freq[:, None] * first_half[None, :] % freq_rows).astype(jnp.float32) * (
        2.0 * math.pi / freq_rows
    )
    angle_turn = (first_freq[:, None] * second_idx[None, :] % grid_total).astype(jnp.float32) * (
        2.0 * math.pi / grid_total
    )
    angle_two = (second_idx[:, None] * second_idx[None, :] % 128).astype(jnp.float32) * (
        2.0 * math.pi / 128
    )
    return (
        jnp.cos(angle_one),
        -jnp.sin(angle_one),
        jnp.cos(angle_turn),
        -jnp.sin(angle_turn),
        jnp.cos(angle_two),
        -jnp.sin(angle_two),
    )


def forward_dft(signal, tables):
    cos_one, sin_one, cos_turn, sin_turn, cos_two, sin_two = tables
    first_re = mult_in("kn,cnm->ckm", cos_one, signal)
    first_im = mult_in("kn,cnm->ckm", sin_one, signal)
    turned_re = first_re * cos_turn - first_im * sin_turn
    turned_im = first_re * sin_turn + first_im * cos_turn
    spec_re = mult_in("ckm,jm->ckj", turned_re, cos_two) - mult_in(
        "ckm,jm->ckj", turned_im, sin_two
    )
    spec_im = mult_in("ckm,jm->ckj", turned_re, sin_two) + mult_in(
        "ckm,jm->ckj", turned_im, cos_two
    )
    return (spec_re, spec_im)


def inverse_dft(spec_re, spec_im, tables):
    cos_one, sin_one, cos_turn, sin_turn, cos_two, sin_two = tables
    grid_total = cos_turn.shape[0] * 128
    first_re = mult_in("ckj,jm->ckm", spec_re, cos_two) + mult_in("ckj,jm->ckm", spec_im, sin_two)
    first_im = mult_in("ckj,jm->ckm", spec_im, cos_two) - mult_in("ckj,jm->ckm", spec_re, sin_two)
    turned_re = first_re * cos_turn + first_im * sin_turn
    turned_im = first_im * cos_turn - first_re * sin_turn
    signal = mult_in("kn,ckm->cnm", cos_one, turned_re) + mult_in("kn,ckm->cnm", sin_one, turned_im)
    return signal * (1.0 / grid_total)


def long_pass(pieces):
    values, grad_pieces, filt_piece = pieces
    item_count = values.shape[1]
    length = values.shape[2]
    half_rows = length // 128
    tables = dft_tables(half_rows)

    def shaped(array):
        return array.reshape(item_count, half_rows, 128)

    def flat(array):
        return array.reshape(1, item_count, length)

    vals_re, vals_im = forward_dft(shaped(values), tables)
    grads_re, grads_im = forward_dft(shaped(grad_pieces), tables)
    filt_re, filt_im = forward_dft(shaped(filt_piece), tables)
    conv_full = inverse_dft(
        vals_re * filt_re - vals_im * filt_im, vals_re * filt_im + vals_im * filt_re, tables
    )
    back_full = inverse_dft(
        filt_re * grads_re + filt_im * grads_im, filt_re * grads_im - filt_im * grads_re, tables
    )
    filter_full = inverse_dft(
        vals_re * grads_re + vals_im * grads_im, vals_re * grads_im - vals_im * grads_re, tables
    )
    return (
        lax.all_to_all(flat(conv_full), "ctx", split_axis=2, concat_axis=0, tiled=True),
        lax.all_to_all(flat(back_full), "ctx", split_axis=2, concat_axis=0, tiled=True),
        lax.all_to_all(flat(filter_full), "ctx", split_axis=2, concat_axis=0, tiled=True),
    )


def to_channel_rows(array, group_count):
    return array.T.reshape(group_count, array.shape[1] // group_count, array.shape[0])


def back_to_tokens(array):
    return array.reshape(array.shape[0] * array.shape[1], array.shape[2]).T


DENSE_TABLE_BYTES = 16 * 2**20


def half_step_table(period, rows):
    halves = period // 2
    steps = (2 * np.arange(halves)[:, None] + 1) * np.arange(rows)[None, :] % (2 * period)
    angle = steps * (math.pi / period)
    return np.concatenate([np.cos(angle), -np.sin(angle)], 0).astype(np.float32)


def to_spec(table, signal):
    return jnp.dot(table, signal, precision=lax.Precision.HIGH)


def from_spec(table, spec):
    signal = lax.dot_general(
        table, spec, (((0,), (0,)), ((), ())), precision=lax.Precision.HIGH
    )
    return signal * (2.0 / table.shape[0])


def times(left, right):
    half = left.shape[0] // 2
    lr, li, rr, ri = left[:half], left[half:], right[:half], right[half:]
    return jnp.concatenate([lr * rr - li * ri, lr * ri + li * rr], 0)


def conj_times(left, right):
    half = left.shape[0] // 2
    lr, li, rr, ri = left[:half], left[half:], right[:half], right[half:]
    return jnp.concatenate([lr * rr + li * ri, lr * ri - li * rr], 0)


def gather_tokens(array):
    return lax.all_to_all(array, "ctx", split_axis=1, concat_axis=0, tiled=True)


def scatter_tokens(array):
    return lax.all_to_all(array, "ctx", split_axis=0, concat_axis=1, tiled=True)


def dense_long_pass(long_in, grad_conv_lr, filter_lr):
    length = long_in.shape[0] * lax.axis_size("ctx")
    table = half_step_table(2 * length, length)
    filt_spec = to_spec(table, gather_tokens(filter_lr))
    grad_spec = to_spec(table, gather_tokens(grad_conv_lr))
    val_spec = to_spec(table, gather_tokens(long_in))
    back = scatter_tokens(from_spec(table, conj_times(filt_spec, grad_spec)))
    conv = scatter_tokens(from_spec(table, times(val_spec, filt_spec)))
    filt = scatter_tokens(from_spec(table, conj_times(val_spec, grad_spec)))
    return conv, back, filt


def split_long_pass(long_in, grad_conv_lr, filter_lr):
    group_count = lax.axis_size("ctx")
    results = long_pass(
        tuple(
            lax.all_to_all(
                to_channel_rows(array, group_count), "ctx", split_axis=0, concat_axis=2, tiled=True
            )
            for array in (long_in, grad_conv_lr, filter_lr)
        )
    )
    return tuple(back_to_tokens(result) for result in results)


def shards(layer_in, query_mr, key_mr, query_lr, key_lr, filter_mr, filter_lr, norm_gain, out_grad):
    row_count, chan_count = layer_in.shape
    tap_count = filter_mr.shape[0]
    full_width = chan_count * lax.axis_size("chan")
    length = row_count * lax.axis_size("ctx")
    medium = half_step_table(row_count + tap_count, row_count + tap_count)
    own_table, next_table = medium[:, :row_count], medium[:, row_count:]
    tap_table = medium[:, :tap_count]
    grad_conv_lr = out_grad * query_lr
    mixed_in = key_mr * layer_in
    preceding = shifted(mixed_in[row_count - tap_count :], "ctx", 1)
    filt_spec = to_spec(tap_table, filter_mr)
    mixed_spec = to_spec(own_table, mixed_in) - to_spec(next_table, preceding)
    conv_mr = from_spec(own_table, times(mixed_spec, filt_spec))
    residual = layer_in + query_mr * conv_mr
    square_sum = lax.psum(jnp.sum(residual * residual, axis=1), "chan")
    inv_rms = lax.rsqrt(square_sum / full_width + 1e-06)[:, None]
    normed = residual * inv_rms * norm_gain
    long_in = key_lr * normed
    dense = 8 * length * length <= DENSE_TABLE_BYTES
    long_form = dense_long_pass if dense else split_long_pass
    conv_lr, grad_long_in, grad_filter_lr = long_form(long_in, grad_conv_lr, filter_lr)
    grad_query_lr = out_grad * conv_lr
    grad_key_lr = grad_long_in * normed
    grad_normed = grad_long_in * key_lr
    gain_part = jnp.sum(grad_normed * residual * inv_rms, axis=0)
    scaled = norm_gain * grad_normed
    cross_sum = lax.psum(jnp.sum(scaled * residual, axis=1), "chan")
    grad_resid = (
        out_grad + inv_rms * scaled - residual * inv_rms**3 * (cross_sum / full_width)[:, None]
    )
    grad_query_mr = grad_resid * conv_mr
    grad_conv_mr = grad_resid * query_mr
    following = shifted(grad_conv_mr[:tap_count], "ctx", -1)
    own_spec = to_spec(own_table, grad_conv_mr)
    filter_part = from_spec(tap_table, conj_times(mixed_spec, own_spec))
    sums = lax.psum(jnp.concatenate([filter_part, gain_part[None]], 0), "ctx")
    grad_filter_mr, grad_gain = sums[:tap_count], sums[tap_count]
    grad_spec = own_spec + to_spec(next_table, following)
    grad_mixed = from_spec(own_table, conj_times(filt_spec, grad_spec))
    grad_key_mr = grad_mixed * layer_in
    grad_in = grad_resid + grad_mixed * key_mr
    return (
        grad_in,
        grad_query_mr,
        grad_key_mr,
        grad_filter_mr,
        grad_gain,
        grad_query_lr,
        grad_key_lr,
        grad_filter_lr,
    )


def solution(mesh):
    in_specs = (
        P("ctx", "chan"),
        P("ctx", "chan"),
        P("ctx", "chan"),
        P("ctx", "chan"),
        P("ctx", "chan"),
        P(None, "chan"),
        P("ctx", "chan"),
        P("chan"),
        P("ctx", "chan"),
    )
    out_specs = (
        P("ctx", "chan"),
        P("ctx", "chan"),
        P("ctx", "chan"),
        P(None, "chan"),
        P("chan"),
        P("ctx", "chan"),
        P("ctx", "chan"),
        P("ctx", "chan"),
    )
    return jax.shard_map(shards, mesh=mesh, in_specs=in_specs, out_specs=out_specs, check_vma=False)
```

```python
import math

import jax
import jax.numpy as jnp
import numpy as np
from jax import lax
from jax.experimental.layout import Layout, with_layout_constraint
from jax.sharding import PartitionSpec as P


def shifted(shard, axis, by):
    peers = lax.axis_size(axis)
    pairs = [(i, i + by) for i in range(peers) if 0 <= i + by < peers]
    return lax.ppermute(shard, axis, pairs)


def mult_in(form, left, right):
    return jnp.einsum(form, left, right, precision=lax.Precision.HIGHEST)


def dft_tables(half_rows):
    freq_rows = 2 * half_rows
    grid_total = freq_rows * 128
    first_freq = jnp.arange(freq_rows, dtype=jnp.int32)
    first_half = jnp.arange(half_rows, dtype=jnp.int32)
    second_idx = jnp.arange(128, dtype=jnp.int32)
    angle_one = (first_freq[:, None] * first_half[None, :] % freq_rows).astype(jnp.float32) * (
        2.0 * math.pi / freq_rows
    )
    angle_turn = (first_freq[:, None] * second_idx[None, :] % grid_total).astype(jnp.float32) * (
        2.0 * math.pi / grid_total
    )
    angle_two = (second_idx[:, None] * second_idx[None, :] % 128).astype(jnp.float32) * (
        2.0 * math.pi / 128
    )
    return (
        jnp.cos(angle_one),
        -jnp.sin(angle_one),
        jnp.cos(angle_turn),
        -jnp.sin(angle_turn),
        jnp.cos(angle_two),
        -jnp.sin(angle_two),
    )


def forward_dft(signal, tables):
    cos_one, sin_one, cos_turn, sin_turn, cos_two, sin_two = tables
    first_re = mult_in("kn,cnm->ckm", cos_one, signal)
    first_im = mult_in("kn,cnm->ckm", sin_one, signal)
    turned_re = first_re * cos_turn - first_im * sin_turn
    turned_im = first_re * sin_turn + first_im * cos_turn
    spec_re = mult_in("ckm,jm->ckj", turned_re, cos_two) - mult_in(
        "ckm,jm->ckj", turned_im, sin_two
    )
    spec_im = mult_in("ckm,jm->ckj", turned_re, sin_two) + mult_in(
        "ckm,jm->ckj", turned_im, cos_two
    )
    return (spec_re, spec_im)


def inverse_dft(spec_re, spec_im, tables):
    cos_one, sin_one, cos_turn, sin_turn, cos_two, sin_two = tables
    grid_total = cos_turn.shape[0] * 128
    first_re = mult_in("ckj,jm->ckm", spec_re, cos_two) + mult_in("ckj,jm->ckm", spec_im, sin_two)
    first_im = mult_in("ckj,jm->ckm", spec_im, cos_two) - mult_in("ckj,jm->ckm", spec_re, sin_two)
    turned_re = first_re * cos_turn + first_im * sin_turn
    turned_im = first_im * cos_turn - first_re * sin_turn
    signal = mult_in("kn,ckm->cnm", cos_one, turned_re) + mult_in("kn,ckm->cnm", sin_one, turned_im)
    return signal * (1.0 / grid_total)


def long_pass(pieces):
    values, grad_pieces, filt_piece = pieces
    item_count = values.shape[1]
    length = values.shape[2]
    half_rows = length // 128
    tables = dft_tables(half_rows)

    def shaped(array):
        return array.reshape(item_count, half_rows, 128)

    def flat(array):
        return array.reshape(1, item_count, length)

    vals_re, vals_im = forward_dft(shaped(values), tables)
    grads_re, grads_im = forward_dft(shaped(grad_pieces), tables)
    filt_re, filt_im = forward_dft(shaped(filt_piece), tables)
    conv_full = inverse_dft(
        vals_re * filt_re - vals_im * filt_im, vals_re * filt_im + vals_im * filt_re, tables
    )
    back_full = inverse_dft(
        filt_re * grads_re + filt_im * grads_im, filt_re * grads_im - filt_im * grads_re, tables
    )
    filter_full = inverse_dft(
        vals_re * grads_re + vals_im * grads_im, vals_re * grads_im - vals_im * grads_re, tables
    )
    return (
        lax.all_to_all(flat(conv_full), "ctx", split_axis=2, concat_axis=0, tiled=True),
        lax.all_to_all(flat(back_full), "ctx", split_axis=2, concat_axis=0, tiled=True),
        lax.all_to_all(flat(filter_full), "ctx", split_axis=2, concat_axis=0, tiled=True),
    )


def to_channel_rows(array, group_count):
    return array.T.reshape(group_count, array.shape[1] // group_count, array.shape[0])


def back_to_tokens(array):
    return array.reshape(array.shape[0] * array.shape[1], array.shape[2]).T


DENSE_TABLE_BYTES = 16 * 2**20


def half_step_table(period, rows):
    halves = period // 2
    steps = (2 * np.arange(halves)[:, None] + 1) * np.arange(rows)[None, :] % (2 * period)
    angle = steps * (math.pi / period)
    return np.concatenate([np.cos(angle), -np.sin(angle)], 0).astype(np.float32)


def to_spec(table, signal):
    return jnp.dot(table, signal, precision=lax.Precision.HIGH)


def from_spec(table, spec):
    back_table = np.ascontiguousarray(table.T * np.float32(2.0 / table.shape[0]))
    return jnp.dot(back_table, spec, precision=lax.Precision.HIGH)


def times(left, right):
    half = left.shape[0] // 2
    lr, li, rr, ri = left[:half], left[half:], right[:half], right[half:]
    return jnp.concatenate([lr * rr - li * ri, lr * ri + li * rr], 0)


def conj_times(left, right):
    half = left.shape[0] // 2
    lr, li, rr, ri = left[:half], left[half:], right[:half], right[half:]
    return jnp.concatenate([lr * rr + li * ri, lr * ri - li * rr], 0)


def rows_first(array):
    return with_layout_constraint(array, Layout(major_to_minor=tuple(range(array.ndim))))


def by_groups(array):
    groups = lax.axis_size("ctx")
    width = array.shape[1] // groups
    array = rows_first(array)
    return jnp.stack([array[:, i * width : (i + 1) * width] for i in range(groups)])


def gather_tokens(array):
    pieces = rows_first(by_groups(array))
    pieces = rows_first(lax.all_to_all(pieces, "ctx", split_axis=0, concat_axis=0))
    return pieces.reshape(-1, pieces.shape[2])


def scatter_tokens(array):
    groups = lax.axis_size("ctx")
    pieces = rows_first(rows_first(array).reshape(groups, -1, array.shape[1]))
    pieces = rows_first(lax.all_to_all(pieces, "ctx", split_axis=0, concat_axis=0))
    return rows_first(jnp.concatenate([pieces[i] for i in range(groups)], 1))


def after(array, *earlier):
    return lax.optimization_barrier((array, *earlier))[0]


def both_tokens(first, second):
    pieces = rows_first(jnp.concatenate([by_groups(first), by_groups(second)], 1))
    pieces = rows_first(lax.all_to_all(pieces, "ctx", split_axis=0, concat_axis=0))
    half = first.shape[0]
    return (
        pieces[:, :half].reshape(-1, pieces.shape[2]),
        pieces[:, half:].reshape(-1, pieces.shape[2]),
    )


def split_long_pass(long_in, grad_conv_lr, filter_lr):
    group_count = lax.axis_size("ctx")
    results = long_pass(
        tuple(
            lax.all_to_all(
                to_channel_rows(array, group_count), "ctx", split_axis=0, concat_axis=2, tiled=True
            )
            for array in (long_in, grad_conv_lr, filter_lr)
        )
    )
    return tuple(back_to_tokens(result) for result in results)


def shards(layer_in, query_mr, key_mr, query_lr, key_lr, filter_mr, filter_lr, norm_gain, out_grad):
    row_count, chan_count = layer_in.shape
    tap_count = filter_mr.shape[0]
    full_width = chan_count * lax.axis_size("chan")
    length = row_count * lax.axis_size("ctx")
    medium = half_step_table(row_count + tap_count, row_count + tap_count)
    own_table, next_table = medium[:, :row_count], medium[:, row_count:]
    tap_table = medium[:, :tap_count]
    grad_conv_lr = out_grad * query_lr
    mixed_in = key_mr * layer_in
    preceding = shifted(mixed_in[row_count - tap_count :], "ctx", 1)
    filt_spec = to_spec(tap_table, filter_mr)
    mixed_spec = to_spec(own_table, mixed_in) - to_spec(next_table, preceding)
    conv_mr = from_spec(own_table, times(mixed_spec, filt_spec))
    dense = 8 * length * length <= DENSE_TABLE_BYTES
    if dense:
        table = half_step_table(2 * length, length)
        filt_all, grad_all = both_tokens(filter_lr, grad_conv_lr)
    residual = layer_in + query_mr * conv_mr
    square_sum = lax.psum(jnp.sum(residual * residual, axis=1), "chan")
    inv_rms = lax.rsqrt(square_sum / full_width + 1e-06)[:, None]
    normed = residual * inv_rms * norm_gain
    long_in = key_lr * normed
    if dense:
        val_all = gather_tokens(after(long_in, filt_all))
        long_filt = to_spec(table, filt_all)
        long_grad = to_spec(table, grad_all)
        back_all = from_spec(table, conj_times(long_filt, long_grad))
        grad_long_in = scatter_tokens(after(back_all, val_all))
        long_val = to_spec(table, val_all)
        conv_all = from_spec(table, times(long_val, long_filt))
        conv_lr = scatter_tokens(after(conv_all, grad_long_in))
    else:
        conv_lr, grad_long_in, grad_filter_lr = split_long_pass(long_in, grad_conv_lr, filter_lr)
    grad_query_lr = out_grad * conv_lr
    grad_key_lr = grad_long_in * normed
    grad_normed = grad_long_in * key_lr
    gain_part = jnp.sum(grad_normed * residual * inv_rms, axis=0)
    scaled = norm_gain * grad_normed
    cross_sum = lax.psum(jnp.sum(scaled * residual, axis=1), "chan")
    grad_resid = (
        out_grad + inv_rms * scaled - residual * inv_rms**3 * (cross_sum / full_width)[:, None]
    )
    grad_query_mr = grad_resid * conv_mr
    grad_conv_mr = grad_resid * query_mr
    following = shifted(grad_conv_mr[:tap_count], "ctx", -1)
    own_spec = to_spec(own_table, grad_conv_mr)
    filter_part = from_spec(tap_table, conj_times(mixed_spec, own_spec))
    spare = jnp.zeros((-(tap_count + 1) % 8, chan_count), jnp.float32)
    parts = jnp.concatenate([filter_part, gain_part[None], spare], 0)
    parts = gather_tokens(after(parts, conv_lr))
    sums = jnp.sum(parts.reshape(lax.axis_size("ctx"), -1, parts.shape[1]), axis=0)
    if dense:
        filt_all = from_spec(table, conj_times(long_val, long_grad))
        grad_filter_lr = scatter_tokens(after(filt_all, parts))
    sums = lax.all_gather(sums, "ctx", axis=1, tiled=True)
    grad_filter_mr, grad_gain = sums[:tap_count], sums[tap_count]
    grad_spec = own_spec + to_spec(next_table, following)
    grad_mixed = from_spec(own_table, conj_times(filt_spec, grad_spec))
    grad_key_mr = grad_mixed * layer_in
    grad_in = grad_resid + grad_mixed * key_mr
    return (
        grad_in,
        grad_query_mr,
        grad_key_mr,
        grad_filter_mr,
        grad_gain,
        grad_query_lr,
        grad_key_lr,
        grad_filter_lr,
    )


def solution(mesh):
    in_specs = (
        P("ctx", "chan"),
        P("ctx", "chan"),
        P("ctx", "chan"),
        P("ctx", "chan"),
        P("ctx", "chan"),
        P(None, "chan"),
        P("ctx", "chan"),
        P("chan"),
        P("ctx", "chan"),
    )
    out_specs = (
        P("ctx", "chan"),
        P("ctx", "chan"),
        P("ctx", "chan"),
        P(None, "chan"),
        P("chan"),
        P("ctx", "chan"),
        P("ctx", "chan"),
        P("ctx", "chan"),
    )
    return jax.shard_map(shards, mesh=mesh, in_specs=in_specs, out_specs=out_specs, check_vma=False)
```

```python
import math

import jax
import jax.numpy as jnp
import numpy as np
from jax import lax
from jax.experimental.layout import Layout, with_layout_constraint
from jax.sharding import PartitionSpec as P


def shifted(shard, axis, by):
    peers = lax.axis_size(axis)
    pairs = [(i, i + by) for i in range(peers) if 0 <= i + by < peers]
    return lax.ppermute(shard, axis, pairs)


def mult_in(form, left, right):
    return jnp.einsum(form, left, right, precision=lax.Precision.HIGHEST)


def dft_tables(half_rows):
    freq_rows = 2 * half_rows
    grid_total = freq_rows * 128
    first_freq = jnp.arange(freq_rows, dtype=jnp.int32)
    first_half = jnp.arange(half_rows, dtype=jnp.int32)
    second_idx = jnp.arange(128, dtype=jnp.int32)
    angle_one = (first_freq[:, None] * first_half[None, :] % freq_rows).astype(jnp.float32) * (
        2.0 * math.pi / freq_rows
    )
    angle_turn = (first_freq[:, None] * second_idx[None, :] % grid_total).astype(jnp.float32) * (
        2.0 * math.pi / grid_total
    )
    angle_two = (second_idx[:, None] * second_idx[None, :] % 128).astype(jnp.float32) * (
        2.0 * math.pi / 128
    )
    return (
        jnp.cos(angle_one),
        -jnp.sin(angle_one),
        jnp.cos(angle_turn),
        -jnp.sin(angle_turn),
        jnp.cos(angle_two),
        -jnp.sin(angle_two),
    )


def forward_dft(signal, tables):
    cos_one, sin_one, cos_turn, sin_turn, cos_two, sin_two = tables
    first_re = mult_in("kn,cnm->ckm", cos_one, signal)
    first_im = mult_in("kn,cnm->ckm", sin_one, signal)
    turned_re = first_re * cos_turn - first_im * sin_turn
    turned_im = first_re * sin_turn + first_im * cos_turn
    spec_re = mult_in("ckm,jm->ckj", turned_re, cos_two) - mult_in(
        "ckm,jm->ckj", turned_im, sin_two
    )
    spec_im = mult_in("ckm,jm->ckj", turned_re, sin_two) + mult_in(
        "ckm,jm->ckj", turned_im, cos_two
    )
    return (spec_re, spec_im)


def inverse_dft(spec_re, spec_im, tables):
    cos_one, sin_one, cos_turn, sin_turn, cos_two, sin_two = tables
    grid_total = cos_turn.shape[0] * 128
    first_re = mult_in("ckj,jm->ckm", spec_re, cos_two) + mult_in("ckj,jm->ckm", spec_im, sin_two)
    first_im = mult_in("ckj,jm->ckm", spec_im, cos_two) - mult_in("ckj,jm->ckm", spec_re, sin_two)
    turned_re = first_re * cos_turn + first_im * sin_turn
    turned_im = first_im * cos_turn - first_re * sin_turn
    signal = mult_in("kn,ckm->cnm", cos_one, turned_re) + mult_in("kn,ckm->cnm", sin_one, turned_im)
    return signal * (1.0 / grid_total)


def long_pass(pieces):
    values, grad_pieces, filt_piece = pieces
    item_count = values.shape[1]
    length = values.shape[2]
    half_rows = length // 128
    tables = dft_tables(half_rows)

    def shaped(array):
        return array.reshape(item_count, half_rows, 128)

    def flat(array):
        return array.reshape(1, item_count, length)

    vals_re, vals_im = forward_dft(shaped(values), tables)
    grads_re, grads_im = forward_dft(shaped(grad_pieces), tables)
    filt_re, filt_im = forward_dft(shaped(filt_piece), tables)
    conv_full = inverse_dft(
        vals_re * filt_re - vals_im * filt_im, vals_re * filt_im + vals_im * filt_re, tables
    )
    back_full = inverse_dft(
        filt_re * grads_re + filt_im * grads_im, filt_re * grads_im - filt_im * grads_re, tables
    )
    filter_full = inverse_dft(
        vals_re * grads_re + vals_im * grads_im, vals_re * grads_im - vals_im * grads_re, tables
    )
    return (
        lax.all_to_all(flat(conv_full), "ctx", split_axis=2, concat_axis=0, tiled=True),
        lax.all_to_all(flat(back_full), "ctx", split_axis=2, concat_axis=0, tiled=True),
        lax.all_to_all(flat(filter_full), "ctx", split_axis=2, concat_axis=0, tiled=True),
    )


def to_channel_rows(array, group_count):
    return array.T.reshape(group_count, array.shape[1] // group_count, array.shape[0])


def back_to_tokens(array):
    return array.reshape(array.shape[0] * array.shape[1], array.shape[2]).T


DENSE_TABLE_BYTES = 16 * 2**20


def half_step_table(period, rows):
    halves = period // 2
    steps = (2 * np.arange(halves)[:, None] + 1) * np.arange(rows)[None, :] % (2 * period)
    angle = steps * (math.pi / period)
    return np.concatenate([np.cos(angle), -np.sin(angle)], 0).astype(np.float32)


def to_spec(table, signal):
    return jnp.dot(table, signal, precision=lax.Precision.HIGH)


def from_spec(table, spec):
    back_table = np.ascontiguousarray(table.T * np.float32(2.0 / table.shape[0]))
    return jnp.dot(back_table, spec, precision=lax.Precision.HIGH)


def times(left, right):
    half = left.shape[0] // 2
    lr, li, rr, ri = left[:half], left[half:], right[:half], right[half:]
    return jnp.concatenate([lr * rr - li * ri, lr * ri + li * rr], 0)


def conj_times(left, right):
    half = left.shape[0] // 2
    lr, li, rr, ri = left[:half], left[half:], right[:half], right[half:]
    return jnp.concatenate([lr * rr + li * ri, lr * ri - li * rr], 0)


def rows_first(array):
    return with_layout_constraint(array, Layout(major_to_minor=tuple(range(array.ndim))))


def by_groups(array):
    groups = lax.axis_size("ctx")
    rows, columns = array.shape
    strip = math.gcd(rows, 8)
    strips = rows_first(array).reshape(rows // strip, strip, groups, columns // groups)
    return strips.transpose(2, 0, 1, 3).reshape(groups, rows, columns // groups)


def gather_tokens(array):
    pieces = rows_first(by_groups(array))
    pieces = rows_first(lax.all_to_all(pieces, "ctx", split_axis=0, concat_axis=0))
    return pieces.reshape(-1, pieces.shape[2])


def scatter_tokens(array):
    groups = lax.axis_size("ctx")
    pieces = rows_first(rows_first(array).reshape(groups, -1, array.shape[1]))
    pieces = rows_first(lax.all_to_all(pieces, "ctx", split_axis=0, concat_axis=0))
    return rows_first(pieces.transpose(1, 0, 2).reshape(pieces.shape[1], -1))


def after(array, earlier):
    return array + 0.0 * earlier[0, 0]


def both_tokens(first, second):
    pieces = rows_first(jnp.concatenate([by_groups(first), by_groups(second)], 1))
    pieces = rows_first(lax.all_to_all(pieces, "ctx", split_axis=0, concat_axis=0))
    half = first.shape[0]
    return (
        pieces[:, :half].reshape(-1, pieces.shape[2]),
        pieces[:, half:].reshape(-1, pieces.shape[2]),
    )


def split_long_pass(long_in, grad_conv_lr, filter_lr):
    group_count = lax.axis_size("ctx")
    results = long_pass(
        tuple(
            lax.all_to_all(
                to_channel_rows(array, group_count), "ctx", split_axis=0, concat_axis=2, tiled=True
            )
            for array in (long_in, grad_conv_lr, filter_lr)
        )
    )
    return tuple(back_to_tokens(result) for result in results)


def shards(layer_in, query_mr, key_mr, query_lr, key_lr, filter_mr, filter_lr, norm_gain, out_grad):
    row_count, chan_count = layer_in.shape
    tap_count = filter_mr.shape[0]
    full_width = chan_count * lax.axis_size("chan")
    length = row_count * lax.axis_size("ctx")
    medium = half_step_table(row_count + tap_count, row_count + tap_count)
    own_table, next_table = medium[:, :row_count], medium[:, row_count:]
    tap_table = medium[:, :tap_count]
    grad_conv_lr = out_grad * query_lr
    mixed_in = key_mr * layer_in
    preceding = shifted(mixed_in[row_count - tap_count :], "ctx", 1)
    filt_spec = to_spec(tap_table, filter_mr)
    mixed_spec = to_spec(own_table, mixed_in) - to_spec(next_table, preceding)
    conv_mr = from_spec(own_table, times(mixed_spec, filt_spec))
    dense = 8 * length * length <= DENSE_TABLE_BYTES
    if dense:
        table = half_step_table(2 * length, length)
        filt_all, grad_all = both_tokens(filter_lr, after(grad_conv_lr, preceding))
    residual = layer_in + query_mr * conv_mr
    square_sum = lax.psum(jnp.sum(residual * residual, axis=1), "chan")
    inv_rms = lax.rsqrt(square_sum / full_width + 1e-06)[:, None]
    normed = residual * inv_rms * norm_gain
    long_in = key_lr * normed
    if dense:
        val_all = gather_tokens(after(long_in, filt_all))
        long_filt = to_spec(table, filt_all)
        long_grad = to_spec(table, grad_all)
        back_all = from_spec(table, conj_times(long_filt, long_grad))
        grad_long_in = scatter_tokens(after(back_all, val_all))
        long_val = to_spec(table, val_all)
        conv_all = from_spec(table, times(long_val, long_filt))
        conv_lr = scatter_tokens(conv_all)
    else:
        conv_lr, grad_long_in, grad_filter_lr = split_long_pass(long_in, grad_conv_lr, filter_lr)
    grad_query_lr = out_grad * conv_lr
    grad_key_lr = grad_long_in * normed
    grad_normed = grad_long_in * key_lr
    gain_part = jnp.sum(grad_normed * residual * inv_rms, axis=0)
    scaled = norm_gain * grad_normed
    cross_sum = lax.psum(jnp.sum(scaled * residual, axis=1), "chan")
    grad_resid = (
        out_grad + inv_rms * scaled - residual * inv_rms**3 * (cross_sum / full_width)[:, None]
    )
    grad_query_mr = grad_resid * conv_mr
    grad_conv_mr = grad_resid * query_mr
    following = shifted(grad_conv_mr[:tap_count], "ctx", -1)
    own_spec = to_spec(own_table, grad_conv_mr)
    filter_part = from_spec(tap_table, conj_times(mixed_spec, own_spec))
    spare = jnp.zeros((-(tap_count + 1) % 8, chan_count), jnp.float32)
    parts = jnp.concatenate([filter_part, gain_part[None], spare], 0)
    parts = gather_tokens(parts)
    sums = jnp.sum(parts.reshape(lax.axis_size("ctx"), -1, parts.shape[1]), axis=0)
    if dense:
        filt_all = from_spec(table, conj_times(long_val, long_grad))
        grad_filter_lr = scatter_tokens(after(filt_all, parts))
    sums = lax.all_gather(sums, "ctx", axis=1, tiled=True)
    grad_filter_mr, grad_gain = sums[:tap_count], sums[tap_count]
    grad_spec = own_spec + to_spec(next_table, following)
    grad_mixed = from_spec(own_table, conj_times(filt_spec, grad_spec))
    grad_key_mr = grad_mixed * layer_in
    grad_in = grad_resid + grad_mixed * key_mr
    return (
        grad_in,
        grad_query_mr,
        grad_key_mr,
        grad_filter_mr,
        grad_gain,
        grad_query_lr,
        grad_key_lr,
        grad_filter_lr,
    )


def solution(mesh):
    in_specs = (
        P("ctx", "chan"),
        P("ctx", "chan"),
        P("ctx", "chan"),
        P("ctx", "chan"),
        P("ctx", "chan"),
        P(None, "chan"),
        P("ctx", "chan"),
        P("chan"),
        P("ctx", "chan"),
    )
    out_specs = (
        P("ctx", "chan"),
        P("ctx", "chan"),
        P("ctx", "chan"),
        P(None, "chan"),
        P("chan"),
        P("ctx", "chan"),
        P("ctx", "chan"),
        P("ctx", "chan"),
    )
    return jax.shard_map(shards, mesh=mesh, in_specs=in_specs, out_specs=out_specs, check_vma=False)
```

```python
import math

import jax
import jax.numpy as jnp
import numpy as np
from jax import lax
from jax.experimental.layout import Layout, with_layout_constraint
from jax.sharding import PartitionSpec as P


def shifted(shard, axis, by):
    peers = lax.axis_size(axis)
    pairs = [(i, i + by) for i in range(peers) if 0 <= i + by < peers]
    return lax.ppermute(shard, axis, pairs)


def mult_in(form, left, right):
    return jnp.einsum(form, left, right, precision=lax.Precision.HIGHEST)


def dft_tables(half_rows):
    freq_rows = 2 * half_rows
    grid_total = freq_rows * 128
    first_freq = jnp.arange(freq_rows, dtype=jnp.int32)
    first_half = jnp.arange(half_rows, dtype=jnp.int32)
    second_idx = jnp.arange(128, dtype=jnp.int32)
    angle_one = (first_freq[:, None] * first_half[None, :] % freq_rows).astype(jnp.float32) * (
        2.0 * math.pi / freq_rows
    )
    angle_turn = (first_freq[:, None] * second_idx[None, :] % grid_total).astype(jnp.float32) * (
        2.0 * math.pi / grid_total
    )
    angle_two = (second_idx[:, None] * second_idx[None, :] % 128).astype(jnp.float32) * (
        2.0 * math.pi / 128
    )
    return (
        jnp.cos(angle_one),
        -jnp.sin(angle_one),
        jnp.cos(angle_turn),
        -jnp.sin(angle_turn),
        jnp.cos(angle_two),
        -jnp.sin(angle_two),
    )


def forward_dft(signal, tables):
    cos_one, sin_one, cos_turn, sin_turn, cos_two, sin_two = tables
    first_re = mult_in("kn,cnm->ckm", cos_one, signal)
    first_im = mult_in("kn,cnm->ckm", sin_one, signal)
    turned_re = first_re * cos_turn - first_im * sin_turn
    turned_im = first_re * sin_turn + first_im * cos_turn
    spec_re = mult_in("ckm,jm->ckj", turned_re, cos_two) - mult_in(
        "ckm,jm->ckj", turned_im, sin_two
    )
    spec_im = mult_in("ckm,jm->ckj", turned_re, sin_two) + mult_in(
        "ckm,jm->ckj", turned_im, cos_two
    )
    return (spec_re, spec_im)


def inverse_dft(spec_re, spec_im, tables):
    cos_one, sin_one, cos_turn, sin_turn, cos_two, sin_two = tables
    grid_total = cos_turn.shape[0] * 128
    first_re = mult_in("ckj,jm->ckm", spec_re, cos_two) + mult_in("ckj,jm->ckm", spec_im, sin_two)
    first_im = mult_in("ckj,jm->ckm", spec_im, cos_two) - mult_in("ckj,jm->ckm", spec_re, sin_two)
    turned_re = first_re * cos_turn + first_im * sin_turn
    turned_im = first_im * cos_turn - first_re * sin_turn
    signal = mult_in("kn,ckm->cnm", cos_one, turned_re) + mult_in("kn,ckm->cnm", sin_one, turned_im)
    return signal * (1.0 / grid_total)


def long_pass(pieces):
    values, grad_pieces, filt_piece = pieces
    item_count = values.shape[1]
    length = values.shape[2]
    half_rows = length // 128
    tables = dft_tables(half_rows)

    def shaped(array):
        return array.reshape(item_count, half_rows, 128)

    def flat(array):
        return array.reshape(1, item_count, length)

    vals_re, vals_im = forward_dft(shaped(values), tables)
    grads_re, grads_im = forward_dft(shaped(grad_pieces), tables)
    filt_re, filt_im = forward_dft(shaped(filt_piece), tables)
    conv_full = inverse_dft(
        vals_re * filt_re - vals_im * filt_im, vals_re * filt_im + vals_im * filt_re, tables
    )
    back_full = inverse_dft(
        filt_re * grads_re + filt_im * grads_im, filt_re * grads_im - filt_im * grads_re, tables
    )
    filter_full = inverse_dft(
        vals_re * grads_re + vals_im * grads_im, vals_re * grads_im - vals_im * grads_re, tables
    )
    return (
        lax.all_to_all(flat(conv_full), "ctx", split_axis=2, concat_axis=0, tiled=True),
        lax.all_to_all(flat(back_full), "ctx", split_axis=2, concat_axis=0, tiled=True),
        lax.all_to_all(flat(filter_full), "ctx", split_axis=2, concat_axis=0, tiled=True),
    )


def to_channel_rows(array, group_count):
    return array.T.reshape(group_count, array.shape[1] // group_count, array.shape[0])


def back_to_tokens(array):
    return array.reshape(array.shape[0] * array.shape[1], array.shape[2]).T


DENSE_TABLE_BYTES = 16 * 2**20


def half_step_table(period, rows):
    halves = period // 2
    steps = (2 * np.arange(halves)[:, None] + 1) * np.arange(rows)[None, :] % (2 * period)
    angle = steps * (math.pi / period)
    return np.concatenate([np.cos(angle), -np.sin(angle)], 0).astype(np.float32)


def to_spec(table, signal):
    return jnp.dot(table, signal, precision=lax.Precision.HIGH)


def from_spec(table, spec):
    back_table = np.ascontiguousarray(table.T * np.float32(2.0 / table.shape[0]))
    return jnp.dot(back_table, spec, precision=lax.Precision.HIGH)


def times(left, right):
    half = left.shape[0] // 2
    lr, li, rr, ri = left[:half], left[half:], right[:half], right[half:]
    return jnp.concatenate([lr * rr - li * ri, lr * ri + li * rr], 0)


def conj_times(left, right):
    half = left.shape[0] // 2
    lr, li, rr, ri = left[:half], left[half:], right[:half], right[half:]
    return jnp.concatenate([lr * rr + li * ri, lr * ri - li * rr], 0)


def rows_first(array):
    return with_layout_constraint(array, Layout(major_to_minor=tuple(range(array.ndim))))


def by_groups(array):
    groups = lax.axis_size("ctx")
    rows, columns = array.shape
    strip = math.gcd(rows, 8)
    strips = rows_first(array).reshape(rows // strip, strip, groups, columns // groups)
    return strips.transpose(2, 0, 1, 3).reshape(groups, rows, columns // groups)


def gather_tokens(array):
    pieces = rows_first(by_groups(array))
    pieces = rows_first(lax.all_to_all(pieces, "ctx", split_axis=0, concat_axis=0))
    return pieces.reshape(-1, pieces.shape[2])


def scatter_tokens(array):
    groups = lax.axis_size("ctx")
    pieces = rows_first(rows_first(array).reshape(groups, -1, array.shape[1]))
    pieces = rows_first(lax.all_to_all(pieces, "ctx", split_axis=0, concat_axis=0))
    return rows_first(pieces.transpose(1, 0, 2).reshape(pieces.shape[1], -1))


def after(array, earlier):
    return array + 0.0 * earlier[0, 0]


def both_tokens(first, second):
    pieces = rows_first(jnp.concatenate([by_groups(first), by_groups(second)], 1))
    pieces = rows_first(lax.all_to_all(pieces, "ctx", split_axis=0, concat_axis=0))
    half = first.shape[0]
    return (
        pieces[:, :half].reshape(-1, pieces.shape[2]),
        pieces[:, half:].reshape(-1, pieces.shape[2]),
    )


def split_long_pass(long_in, grad_conv_lr, filter_lr):
    group_count = lax.axis_size("ctx")
    results = long_pass(
        tuple(
            lax.all_to_all(
                to_channel_rows(array, group_count), "ctx", split_axis=0, concat_axis=2, tiled=True
            )
            for array in (long_in, grad_conv_lr, filter_lr)
        )
    )
    return tuple(back_to_tokens(result) for result in results)


def shards(layer_in, query_mr, key_mr, query_lr, key_lr, filter_mr, filter_lr, norm_gain, out_grad):
    row_count, chan_count = layer_in.shape
    tap_count = filter_mr.shape[0]
    full_width = chan_count * lax.axis_size("chan")
    length = row_count * lax.axis_size("ctx")
    medium = half_step_table(row_count + tap_count, row_count + tap_count)
    own_table, next_table = medium[:, :row_count], medium[:, row_count:]
    tap_table = medium[:, :tap_count]
    grad_conv_lr = out_grad * query_lr
    mixed_in = key_mr * layer_in
    preceding = shifted(mixed_in[row_count - tap_count :], "ctx", 1)
    dense = 8 * length * length <= DENSE_TABLE_BYTES
    if dense:
        table = half_step_table(2 * length, length)
        filt_all, grad_all = both_tokens(filter_lr, grad_conv_lr)
        long_filt = to_spec(table, filt_all)
        long_grad = to_spec(table, grad_all)
        back_all = from_spec(table, conj_times(long_filt, long_grad))
        grad_long_in = scatter_tokens(back_all)
        preceding = after(preceding, back_all)
    filt_spec = to_spec(tap_table, filter_mr)
    mixed_spec = to_spec(own_table, mixed_in) - to_spec(next_table, preceding)
    conv_mr = from_spec(own_table, times(mixed_spec, filt_spec))
    residual = layer_in + query_mr * conv_mr
    square_sum = lax.psum(jnp.sum(residual * residual, axis=1), "chan")
    inv_rms = lax.rsqrt(square_sum / full_width + 1e-06)[:, None]
    normed = residual * inv_rms * norm_gain
    long_in = key_lr * normed
    if dense:
        val_all = gather_tokens(after(long_in, grad_long_in))
    else:
        conv_lr, grad_long_in, grad_filter_lr = split_long_pass(long_in, grad_conv_lr, filter_lr)
    grad_key_lr = grad_long_in * normed
    grad_normed = grad_long_in * key_lr
    gain_part = jnp.sum(grad_normed * residual * inv_rms, axis=0)
    scaled = norm_gain * grad_normed
    cross_sum = lax.psum(jnp.sum(scaled * residual, axis=1), "chan")
    grad_resid = (
        out_grad + inv_rms * scaled - residual * inv_rms**3 * (cross_sum / full_width)[:, None]
    )
    grad_query_mr = grad_resid * conv_mr
    grad_conv_mr = grad_resid * query_mr
    following = shifted(grad_conv_mr[:tap_count], "ctx", -1)
    own_spec = to_spec(own_table, grad_conv_mr)
    filter_part = from_spec(tap_table, conj_times(mixed_spec, own_spec))
    spare = jnp.zeros((-(tap_count + 1) % 8, chan_count), jnp.float32)
    parts = jnp.concatenate([filter_part, gain_part[None], spare], 0)
    if dense:
        parts = after(parts, val_all)
        long_val = to_spec(table, after(val_all, parts))
    totals = gather_tokens(parts)
    sums = jnp.sum(totals.reshape(lax.axis_size("ctx"), -1, totals.shape[1]), axis=0)
    if dense:
        conv_all = from_spec(table, times(long_val, long_filt))
        conv_lr = scatter_tokens(after(conv_all, totals))
        filt_all = from_spec(table, conj_times(long_val, long_grad))
        grad_filter_lr = scatter_tokens(after(filt_all, conv_lr))
    grad_query_lr = out_grad * conv_lr
    sums = lax.all_gather(sums, "ctx", axis=1, tiled=True)
    grad_filter_mr, grad_gain = sums[:tap_count], sums[tap_count]
    grad_spec = own_spec + to_spec(next_table, following)
    grad_mixed = from_spec(own_table, conj_times(filt_spec, grad_spec))
    grad_key_mr = grad_mixed * layer_in
    grad_in = grad_resid + grad_mixed * key_mr
    return (
        grad_in,
        grad_query_mr,
        grad_key_mr,
        grad_filter_mr,
        grad_gain,
        grad_query_lr,
        grad_key_lr,
        grad_filter_lr,
    )


def solution(mesh):
    in_specs = (
        P("ctx", "chan"),
        P("ctx", "chan"),
        P("ctx", "chan"),
        P("ctx", "chan"),
        P("ctx", "chan"),
        P(None, "chan"),
        P("ctx", "chan"),
        P("chan"),
        P("ctx", "chan"),
    )
    out_specs = (
        P("ctx", "chan"),
        P("ctx", "chan"),
        P("ctx", "chan"),
        P(None, "chan"),
        P("chan"),
        P("ctx", "chan"),
        P("ctx", "chan"),
        P("ctx", "chan"),
    )
    return jax.shard_map(shards, mesh=mesh, in_specs=in_specs, out_specs=out_specs, check_vma=False)
```
